32 devices in a mesh: mp: 2 (over y), gx: 8 (over z, x), gy: 2 (over core).
Axes of the slice: x: 2, y: 2, z: 4, core: 2. Of those that a mesh axis runs over, the one named last changes fastest.
Arguments:
- tracers: float32 [16, 60, 128, 512], P(None, None, 'gx', ('mp', 'gy')), may hold values from -6 to 6
- wind_courant: float32 [2, 60, 128, 512], P(None, None, 'gx', ('mp', 'gy')), may hold values from -0.45 to 0.45
- pressure_head: float32 [8, 128, 512], P(None, ('gx', 'gy'), 'mp'), may hold values from -2 to 0.5
- storage: float32 [8, 128, 512], P(None, ('gx', 'gy'), 'mp'), may hold values from 0.05 to 0.5
- soil_type: int32 [128, 512], P(('gx', 'gy'), 'mp'), may hold values from 0 to 11
- land_mask: int32 [128, 512], P(('gx', 'gy'), 'mp'), may hold values 0 or 1
- conductivity_table: float32 [12], replicated, may hold values from 0.3 to 3
- exponent_table: float32 [12], replicated, may hold values from 0.2 to 1
Outputs:
- tracers_out: float32 [16, 60, 128, 512], P(None, None, 'gx', ('mp', 'gy'))
- new_head: float32 [8, 128, 512], P(None, ('gx', 'gy'), 'mp')
The draws below stay inside these ranges and needn't reach their ends.
All inputs are finite; a program needn't handle non-finite values. No bound on the sum of `land_mask` on one device may be relied on, other than what follows from the above.
Results may differ from the reference program's by a relative error of at most 0.00002.
Values sent between devices are 32-bit elements; how exact they have to be, the bound alone decides.
A program may use at most 256 MiB of HBM per device.

```python
import math
import jax
import jax.numpy as jnp
from jax import lax

LEV = 60
NTR = 16
LAY = 8
NSOIL = 12
STEPS = 2
SWEEPS = 3
NXL = 128
NW = 512


def with_ends(values, rng, least, largest):
    shape = values.shape
    index_at = [jax.random.randint(jax.random.fold_in(rng, axis), (), 0, shape[axis]) for axis in range(len(shape))]
    values = values.at[tuple(index_at)].set(least)
    longest = shape.index(max(shape))
    index_at[longest] = (index_at[longest] + 1) % shape[longest]
    return values.at[tuple(index_at)].set(largest)


def shard_levels(own_key, dims, pieces, least, largest):
    factor_of = 1.0
    for position, shards_of in pieces:
        steps = jax.random.uniform(jax.random.fold_in(jax.random.fold_in(own_key, 6), position), (shards_of,), jnp.float32, least / len(pieces), largest / len(pieces))
        factor_of = factor_of * jnp.repeat(jnp.exp(steps), dims[position] // shards_of).reshape((-1,) + (1,) * (len(dims) - 1 - position))
    return factor_of


def gaussian(rng, shape, width, bound, pieces=(), kind=jnp.bfloat16):
    result = jax.random.normal(rng, shape, jnp.float32) * width
    if len(pieces) > 0:
        result = shard_levels(rng, shape, pieces, -0.22, 0.18) * result
    return jnp.clip(result, min=-bound, max=bound).astype(kind)


def setup_inputs(seed: int = 0) -> dict:
    streams_of = jax.random.split(jax.random.key(seed), 9)
    tracers = gaussian(streams_of[0], (NTR, LEV, NXL, NW), 1.0, 6.0, ((2, 8), (3, 4)), jnp.float32)
    wind_courant = jnp.clip(jax.random.uniform(streams_of[1], (2, LEV, NXL, NW), jnp.float32, -0.45, 0.45) * shard_levels(streams_of[1], (2, LEV, NXL, NW), ((2, 8), (3, 4)), -0.4, 0.0), -0.45, 0.45)
    pressure_head = jnp.clip(-2.0 + 2.5 * jax.random.uniform(streams_of[2], (LAY, NXL, NW), jnp.float32) ** shard_levels(streams_of[2], (LAY, NXL, NW), ((1, 16), (2, 2)), -0.2, 0.2), -2.0, 0.5)
    storage = jnp.clip(jnp.exp(math.log(0.5) - 2.3025851 * jax.random.uniform(streams_of[3], (LAY, NXL, NW), jnp.float32) ** shard_levels(streams_of[3], (LAY, NXL, NW), ((1, 16), (2, 2)), -0.2, 0.2)), 0.05, 0.5)
    soil_type = with_ends(jax.random.randint(streams_of[4], (NXL, NW), 0, NSOIL), jax.random.fold_in(streams_of[4], 1), 0, NSOIL - 1).astype(jnp.int32)
    land_mask = with_ends((jax.random.randint(streams_of[5], (NXL, NW), 0, 4) < 3).astype(jnp.int32), jax.random.fold_in(streams_of[5], 1), 0, 1)
    conductivity_table = jnp.clip(jnp.exp(jax.random.uniform(streams_of[6], (NSOIL,), jnp.float32, math.log(0.3), math.log(3.0))), 0.3, 3.0)
    exponent_table = jnp.clip(jnp.exp(jax.random.uniform(streams_of[7], (NSOIL,), jnp.float32, math.log(0.2), math.log(1.0))), 0.2, 1.0)
    return {"tracers": tracers, "wind_courant": wind_courant, "pressure_head": pressure_head, "storage": storage, "soil_type": soil_type, "land_mask": land_mask, "conductivity_table": conductivity_table, "exponent_table": exponent_table}


def advect(padded, wind_along, wind_across):
    mid_field = padded[..., 1:-1]
    mid_wind = wind_along[..., 1:-1]
    flux_along = jnp.maximum(mid_wind[..., :-1, :], 0.0) * mid_field[..., :-1, :] + jnp.minimum(mid_wind[..., 1:, :], 0.0) * mid_field[..., 1:, :]
    row_field = padded[..., 1:-1, :]
    row_wind = wind_across[..., 1:-1, :]
    flux_across = jnp.maximum(row_wind[..., :-1], 0.0) * row_field[..., :-1] + jnp.minimum(row_wind[..., 1:], 0.0) * row_field[..., 1:]
    center = padded[..., 1:-1, 1:-1]
    return center - (flux_along[..., 1:, :] - flux_along[..., :-1, :]) - (flux_across[..., 1:] - flux_across[..., :-1])


def harmonic(first_cond, second_cond):
    return 2.0 * first_cond * second_cond / (first_cond + second_cond)


def sweep(padded, saturated, exponent, capacity, previous, surface):
    conductance = saturated * jnp.exp(exponent * jnp.minimum(padded, 0.0))
    center = conductance[:, 1:-1, 1:-1]
    iterate = padded[:, 1:-1, 1:-1]
    east_face = harmonic(center, conductance[:, 2:, 1:-1])
    west_face = harmonic(center, conductance[:, :-2, 1:-1])
    north_face = harmonic(center, conductance[:, 1:-1, 2:])
    south_face = harmonic(center, conductance[:, 1:-1, :-2])
    lateral = east_face * padded[:, 2:, 1:-1] + west_face * padded[:, :-2, 1:-1] + north_face * padded[:, 1:-1, 2:] + south_face * padded[:, 1:-1, :-2]
    vertical = harmonic(center[:-1], center[1:])
    blank_layer = jnp.zeros_like(center[:1])
    below_face = jnp.concatenate([vertical, blank_layer], axis=0)
    above_face = jnp.concatenate([blank_layer, vertical], axis=0)
    inflow = jnp.concatenate([surface[None], jnp.zeros_like(center[1:])], axis=0)
    drainage = jnp.concatenate([jnp.zeros_like(center[:-1]), center[-1:]], axis=0)
    denominator = capacity + east_face + west_face + north_face + south_face + above_face + below_face
    numerator = capacity * previous + lateral + above_face * jnp.concatenate([blank_layer, iterate[:-1]], axis=0) + below_face * jnp.concatenate([iterate[1:], blank_layer], axis=0) + above_face - below_face + inflow - drainage
    return numerator / denominator


def lookup(soil_kinds, values_table):
    matches = soil_kinds[None] == jnp.arange(values_table.shape[0], dtype=jnp.int32)[:, None, None]
    return jnp.sum(jnp.where(matches, values_table[:, None, None], jnp.float32(0.0)), axis=0)


def pad_cells(field):
    spec = [(0, 0)] * (field.ndim - 2) + [(1, 1), (1, 1)]
    return jnp.pad(field, spec)


def reference(tracers, wind_courant, pressure_head, storage, soil_type, land_mask, conductivity_table, exponent_table):
    wind_along = pad_cells(wind_courant[0])
    wind_across = pad_cells(wind_courant[1])

    def all_steps(field):
        for repeat in range(STEPS):
            field = advect(pad_cells(field), wind_along, wind_across)
        return field

    tracers_out = lax.map(all_steps, tracers)
    precip = jax.nn.softplus(tracers_out[3, 0])
    evaporation = jax.nn.softplus(-tracers_out[1, 0])
    radiation = jax.nn.sigmoid(tracers_out[0, 0]) * jnp.exp(-jax.nn.softplus(tracers_out[2, 0]))
    surface = land_mask.astype(jnp.float32) * (precip - evaporation * radiation)
    saturated = pad_cells(lookup(soil_type, conductivity_table))
    exponent = pad_cells(lookup(soil_type, exponent_table))
    iterate = pressure_head
    for repeat in range(SWEEPS):
        iterate = sweep(pad_cells(iterate), saturated, exponent, storage, pressure_head, surface)
    return tracers_out, iterate
```

```python
import functools

import jax
import jax.numpy as jnp
from jax import lax
from jax.experimental import pallas as pl
from jax.experimental.pallas import tpu as pltpu
from jax.sharding import PartitionSpec as P

SWEEPS = 3
MESH = pl.DeviceIdType.MESH
UP, DOWN, RIGHT, LEFT = range(4)


def softplus(value):
    return jnp.maximum(value, 0.0) + jnp.log(1.0 + jnp.exp(-jnp.abs(value)))


def harmonic(first_cond, second_cond):
    summed = first_cond + second_cond
    return 2.0 * first_cond * second_cond / jnp.where(summed > 0.0, summed, 1.0)


def kernel(
    sizes,
    tracers_hbm,
    wind_hbm,
    head_hbm,
    storage_hbm,
    type_hbm,
    mask_hbm,
    cond_table,
    exp_table,
    out_hbm,
    head_out_hbm,
    q,
    wind,
    row_send,
    row_recv,
    col_send,
    col_recv,
    head,
    storage,
    soil_type,
    mask,
    saturated,
    exponent,
    iterate,
    cond,
    surface_send,
    surface,
    edge_send,
    edge_recv,
    side_send,
    side_recv,
    load_sem,
    soil_sem,
    store_sem,
    send_sem,
    recv_sem,
    edge_send_sem,
    edge_recv_sem,
    surface_sem,
    head_sem,
):
    n_mp, n_gx, n_gy, chunk = sizes
    species, levels, rows, cols = tracers_hbm.shape
    layers, soil_rows, soil_cols = head_hbm.shape
    chunks = levels // chunk
    mp, gx, gy = lax.axis_index("mp"), lax.axis_index("gx"), lax.axis_index("gy")
    across = mp * n_gy + gy
    along = gx * n_gy + gy
    n_across, n_along = n_mp * n_gy, n_gx * n_gy

    def across_device(index):
        return (index // n_gy, gx, lax.rem(index, n_gy))

    def along_device(index):
        return (mp, index // n_gy, lax.rem(index, n_gy))

    sends = (gx < n_gx - 1, gx > 0, across < n_across - 1, across > 0)
    gets = (gx > 0, gx < n_gx - 1, across > 0, across < n_across - 1)
    targets = (
        (mp, gx + 1, gy),
        (mp, gx - 1, gy),
        across_device(across + 1),
        across_device(across - 1),
    )

    def load(c):
        part = pl.ds(c * chunk, chunk)
        return (
            pltpu.make_async_copy(wind_hbm.at[:, part], wind.at[:, part], load_sem.at[0, c]),
            pltpu.make_async_copy(tracers_hbm.at[:, part], q.at[:, part], load_sem.at[1, c]),
        )

    def store(c):
        part = pl.ds(c * chunk, chunk)
        return pltpu.make_async_copy(q.at[:, part], out_hbm.at[:, part], store_sem.at[c])

    @pl.loop(0, chunks)
    def _(c):
        for copy in load(c):
            copy.start()

    soil_loads = [
        pltpu.make_async_copy(source, target, soil_sem.at[place])
        for place, (source, target) in enumerate(
            ((head_hbm, head), (storage_hbm, storage), (type_hbm, soil_type), (mask_hbm, mask))
        )
    ]
    for copy in soil_loads:
        copy.start()

    barrier = pltpu.get_barrier_semaphore()
    other_chip = lax.rem(mp + 1, n_mp)
    greeted = list(zip(sends, targets)) + [
        (jnp.logical_and(along > 0, gy == 0), along_device(along - 1)),
        (jnp.logical_and(along < n_along - 1, gy == n_gy - 1), along_device(along + 1)),
        (mp >= 0, (other_chip, gx, gy)),
    ]
    for there, device in greeted:

        @pl.when(there)
        def _(device=device):
            pl.semaphore_signal(barrier, inc=1, device_id=device, device_id_type=MESH)

    pl.semaphore_wait(barrier, sum(there.astype(jnp.int32) for there, _ in greeted))

    for way in range(4):
        place = row_recv if way < 2 else col_recv

        @pl.when(jnp.logical_not(gets[way]))
        def _(place=place, way=way):
            place[:, way % 2] = jnp.zeros_like(place[:, way % 2])

    def transfer(c, turn, way):
        part = pl.ds(c * chunk, chunk)
        source, target = (row_send, row_recv) if way < 2 else (col_send, col_recv)
        return pltpu.make_async_remote_copy(
            src_ref=source.at[turn, way % 2, part],
            dst_ref=target.at[turn, way % 2, part],
            send_sem=send_sem.at[turn, way, c],
            recv_sem=recv_sem.at[turn, way, c],
            device_id=targets[way],
            device_id_type=MESH,
        )

    def start(c, turn):
        for way in range(4):

            @pl.when(sends[way])
            def _(way=way):
                transfer(c, turn, way).start()

    def arrive(c, turn):
        for way in range(4):

            @pl.when(gets[way])
            def _(way=way):
                transfer(c, turn, way).wait_recv()

    lane = lax.broadcasted_iota(jnp.int32, (rows, cols), 1)
    row = lax.broadcasted_iota(jnp.int32, (rows, cols), 0)

    def winds(level):
        u, v = wind[0, level], wind[1, level]
        return jnp.maximum(u, 0.0), jnp.minimum(u, 0.0), jnp.maximum(v, 0.0), jnp.minimum(v, 0.0)

    def pack(level, turn, kind, field, parts, packed):
        u_pos, u_neg, v_pos, v_neg = parts
        right, left = packed
        row_send[turn, UP, level, kind : kind + 1] = (u_pos * field)[rows - 1 : rows]
        row_send[turn, DOWN, level, kind : kind + 1] = (u_neg * field)[0:1]
        right = jnp.where(
            lane == kind, pltpu.roll(v_pos * field, (kind + 1) % cols, 1), right
        )
        left_part = v_neg * field
        if kind > 0:
            left_part = pltpu.roll(left_part, kind, 1)
        left = jnp.where(lane == kind, left_part, left)
        return right, left

    def pack_done(level, turn, packed):
        col_send[turn, 0, level] = packed[0]
        col_send[turn, 1, level] = packed[1]

    def blank():
        return (jnp.zeros((rows, cols), jnp.float32),) * 2

    def advance(level, turn, kind, parts):
        u_pos, u_neg, v_pos, v_neg = parts
        field = q[kind, level]
        plus, minus = u_pos * field, u_neg * field
        above = row_recv[turn, DOWN, level, kind : kind + 1]
        below = row_recv[turn, UP, level, kind : kind + 1]
        face = plus + jnp.where(row == rows - 1, above, pltpu.roll(minus, rows - 1, 0))
        face_before = jnp.where(row == 0, below + minus, pltpu.roll(face, 1, 0))
        plus, minus = v_pos * field, v_neg * field
        from_left = col_recv[turn, 0, level]
        if kind > 0:
            from_left = pltpu.roll(from_left, cols - kind, 1)
        from_right = pltpu.roll(col_recv[turn, 1, level], cols - 1 - kind, 1)
        side = plus + jnp.where(lane == cols - 1, from_right, pltpu.roll(minus, cols - 1, 1))
        side_before = jnp.where(lane == 0, from_left, pltpu.roll(plus, 1, 1)) + minus
        return field - (face - face_before) - (side - side_before)

    def first_edges(c):
        @pl.loop(c * chunk, (c + 1) * chunk)
        def _(level):
            parts, packed = winds(level), blank()
            for kind in range(species):
                packed = pack(level, 0, kind, q[kind, level], parts, packed)
            pack_done(level, 0, packed)

    def first_step(c):
        @pl.loop(c * chunk, (c + 1) * chunk)
        def _(level):
            parts, packed = winds(level), blank()
            for kind in range(species):
                field = advance(level, 0, kind, parts)
                packed = pack(level, 1, kind, field, parts, packed)
                q[kind, level] = field
            pack_done(level, 1, packed)

    def second_step(c):
        @pl.loop(c * chunk, (c + 1) * chunk)
        def _(level):
            parts = winds(level)
            for kind in range(species):
                q[kind, level] = advance(level, 1, kind, parts)

    edge_sends = (along < n_along - 1, along > 0, mp >= 0)
    edge_gets = (along > 0, along < n_along - 1, mp >= 0)
    edge_targets = (along_device(along + 1), along_device(along - 1), (other_chip, gx, gy))
    half = soil_cols // 2

    def edge_transfer(turn, way):
        source, target = (
            (edge_send.at[turn, way], edge_recv.at[turn, way])
            if way < 2
            else (side_send.at[turn], side_recv.at[turn])
        )
        return pltpu.make_async_remote_copy(
            src_ref=source,
            dst_ref=target,
            send_sem=edge_send_sem.at[turn, way],
            recv_sem=edge_recv_sem.at[turn, way],
            device_id=edge_targets[way],
            device_id_type=MESH,
        )

    def soil_edges(turn):
        for layer in range(layers):
            values = iterate[layer]
            conds = saturated[...] * jnp.exp(exponent[...] * jnp.minimum(values, 0.0))
            cond[layer] = conds
            for place, array in enumerate((values, conds)):
                edge_send[turn, 0, place, layer : layer + 1] = array[soil_rows - 1 : soil_rows]
                edge_send[turn, 1, place, layer : layer + 1] = array[0:1]
                side_send[turn, place, layer] = jnp.where(mp == 0, array[:, half:], array[:, :half])
        for way in range(3):

            @pl.when(edge_sends[way])
            def _(way=way):
                edge_transfer(turn, way).start()

    soil_row = lax.broadcasted_iota(jnp.int32, (soil_rows, soil_cols), 0)
    soil_lane = lax.broadcasted_iota(jnp.int32, (soil_rows, soil_cols), 1)

    def soil_sweep(turn):
        for way in range(3):

            @pl.when(edge_gets[way])
            def _(way=way):
                edge_transfer(turn, way).wait_recv()

        def neighbours(place, layer, array):
            low = edge_recv[turn, 0, place, layer : layer + 1]
            high = edge_recv[turn, 1, place, layer : layer + 1]
            side = side_recv[turn, place, layer]
            side = jnp.concatenate([side, side], axis=1)
            left_end = jnp.where(mp == 0, 0.0, pltpu.roll(side, 1, 1))
            right_end = jnp.where(mp == n_mp - 1, 0.0, pltpu.roll(side, soil_cols - 1, 1))
            return (
                jnp.where(soil_row == 0, low, pltpu.roll(array, 1, 0)),
                jnp.where(soil_row == soil_rows - 1, high, pltpu.roll(array, soil_rows - 1, 0)),
                jnp.where(soil_lane == 0, left_end, pltpu.roll(array, 1, 1)),
                jnp.where(soil_lane == soil_cols - 1, right_end, pltpu.roll(array, soil_cols - 1, 1)),
            )

        values = [iterate[layer] for layer in range(layers)]
        below_faces = [harmonic(cond[i], cond[i + 1]) for i in range(layers - 1)]
        for layer in range(layers):
            center = cond[layer]
            capacity = storage[layer]
            top, bottom = capacity * head[layer], capacity
            for near_cond, near in zip(
                neighbours(1, layer, center), neighbours(0, layer, values[layer])
            ):
                face = harmonic(center, near_cond)
                top = top + face * near
                bottom = bottom + face
            if layer > 0:
                face = below_faces[layer - 1]
                top = top + face * values[layer - 1] + face
                bottom = bottom + face
            if layer < layers - 1:
                face = below_faces[layer]
                top = top + face * values[layer + 1] - face
                bottom = bottom + face
            if layer == 0:
                top = top + mask[...].astype(jnp.float32) * surface[...]
            if layer == layers - 1:
                top = top - center
            iterate[layer] = top / bottom

    def soil_start():
        for copy in soil_loads:
            copy.wait()
        kinds = soil_type[...]
        for target, table in ((saturated, cond_table), (exponent, exp_table)):
            found = jnp.zeros(kinds.shape, jnp.float32)
            for kind in range(table.shape[0]):
                found = jnp.where(kinds == kind, table[kind], found)
            target[...] = found
        for way in range(2):

            @pl.when(jnp.logical_not(edge_gets[way]))
            def _(way=way):
                edge_recv[:, way] = jnp.zeros_like(edge_recv[:, way])

        iterate[...] = head[...]
        soil_edges(0)

    def surface_transfer(core):
        return pltpu.make_async_remote_copy(
            src_ref=surface_send,
            dst_ref=surface.at[:, pl.ds(core * cols, cols)],
            send_sem=surface_sem.at[0],
            recv_sem=surface_sem.at[1],
            device_id=(mp, gx, 1 - gy),
            device_id_type=MESH,
        )

    def surface_start():
        precip = softplus(q[3, 0])
        evaporation = softplus(-q[1, 0])
        radiation = jnp.exp(-softplus(q[2, 0])) / (1.0 + jnp.exp(-q[0, 0]))
        field = precip - evaporation * radiation
        for core in range(2):

            @pl.when(gy == core)
            def _(core=core):
                other = 1 - core
                surface[:, core * cols : (core + 1) * cols] = field[
                    core * soil_rows : (core + 1) * soil_rows
                ]
                surface_send[...] = field[other * soil_rows : (other + 1) * soil_rows]
                surface_transfer(core).start()

    def surface_wait():
        for core in range(2):

            @pl.when(gy == core)
            def _(core=core):
                surface_transfer(1 - core).wait_recv()
                surface_transfer(core).wait_send()

    head_store = pltpu.make_async_copy(iterate, head_out_hbm, head_sem.at[0])

    @pl.loop(0, chunks + 2)
    def _(turn):
        @pl.when(turn < chunks)
        def _():
            for copy in load(turn):
                copy.wait()
            first_edges(turn)
            start(turn, 0)

        @pl.when(turn == 0)
        def _():
            soil_start()

        @pl.when(jnp.logical_and(turn >= 1, turn <= chunks))
        def _():
            arrive(turn - 1, 0)
            first_step(turn - 1)
            start(turn - 1, 1)

        @pl.when(turn >= 2)
        def _():
            arrive(turn - 2, 1)
            second_step(turn - 2)
            store(turn - 2).start()

        @pl.when(turn == 2)
        def _():
            surface_start()

        @pl.when(turn == 4)
        def _():
            surface_wait()
            soil_sweep(0)
            soil_edges(1)

        @pl.when(turn == 6)
        def _():
            soil_sweep(1)
            soil_edges(2)

        @pl.when(turn == 8)
        def _():
            soil_sweep(2)
            head_store.start()

    for turn in range(SWEEPS):
        for way in range(3):

            @pl.when(edge_sends[way])
            def _(turn=turn, way=way):
                edge_transfer(turn, way).wait_send()

    head_store.wait()

    @pl.loop(0, chunks)
    def _(c):
        for turn in range(2):
            for way in range(4):

                @pl.when(sends[way])
                def _(turn=turn, way=way):
                    transfer(c, turn, way).wait_send()

        store(c).wait()


def on_device(sizes, *arguments):
    tracers, wind, head = arguments[:3]
    species, levels, rows, cols = tracers.shape
    layers, soil_rows, soil_cols = head.shape
    chunk = next(c for c in (6, 5, 4, 3, 2, 1) if levels % c == 0)
    chunks = levels // chunk
    f32 = jnp.float32
    anywhere = pl.BlockSpec(memory_space=pl.ANY)
    scalars = pl.BlockSpec(memory_space=pltpu.SMEM)
    soil = (layers, soil_rows, soil_cols)
    return pl.pallas_call(
        functools.partial(kernel, sizes + (chunk,)),
        out_shape=(
            jax.ShapeDtypeStruct(tracers.shape, f32),
            jax.ShapeDtypeStruct(head.shape, f32),
        ),
        in_specs=[pl.BlockSpec(memory_space=pltpu.HBM)] * 6 + [scalars] * 2,
        out_specs=(anywhere, anywhere),
        scratch_shapes=[
            pltpu.VMEM(tracers.shape, f32),
            pltpu.VMEM(wind.shape, f32),
            pltpu.VMEM((2, 2, levels, species, cols), f32),
            pltpu.VMEM((2, 2, levels, species, cols), f32),
            pltpu.VMEM((2, 2, levels, rows, cols), f32),
            pltpu.VMEM((2, 2, levels, rows, cols), f32),
            pltpu.VMEM(soil, f32),
            pltpu.VMEM(soil, f32),
            pltpu.VMEM(soil[1:], jnp.int32),
            pltpu.VMEM(soil[1:], jnp.int32),
            pltpu.VMEM(soil[1:], f32),
            pltpu.VMEM(soil[1:], f32),
            pltpu.VMEM(soil, f32),
            pltpu.VMEM(soil, f32),
            pltpu.VMEM((soil_rows, cols), f32),
            pltpu.VMEM((soil_rows, soil_cols), f32),
            pltpu.VMEM((SWEEPS, 2, 2, layers, soil_cols), f32),
            pltpu.VMEM((SWEEPS, 2, 2, layers, soil_cols), f32),
            pltpu.VMEM((SWEEPS, 2, layers, soil_rows, soil_cols // 2), f32),
            pltpu.VMEM((SWEEPS, 2, layers, soil_rows, soil_cols // 2), f32),
            pltpu.SemaphoreType.DMA((2, chunks)),
            pltpu.SemaphoreType.DMA((4,)),
            pltpu.SemaphoreType.DMA((chunks,)),
            pltpu.SemaphoreType.DMA((2, 4, chunks)),
            pltpu.SemaphoreType.DMA((2, 4, chunks)),
            pltpu.SemaphoreType.DMA((SWEEPS, 3)),
            pltpu.SemaphoreType.DMA((SWEEPS, 3)),
            pltpu.SemaphoreType.DMA((2,)),
            pltpu.SemaphoreType.DMA((1,)),
        ],
        compiler_params=pltpu.CompilerParams(
            collective_id=0, has_side_effects=True, vmem_limit_bytes=28 * 1024 * 1024
        ),
    )(*arguments)


def solution(mesh):
    tall, flat = P(None, None, "gx", ("mp", "gy")), P(None, ("gx", "gy"), "mp")
    ground = P(("gx", "gy"), "mp")
    sizes = (mesh.shape["mp"], mesh.shape["gx"], mesh.shape["gy"])
    return jax.shard_map(
        functools.partial(on_device, sizes),
        mesh=mesh,
        in_specs=(tall, tall, flat, flat, ground, ground, P(), P()),
        out_specs=(tall, flat),
        check_vma=False,
    )
```

```python
import functools

import jax
import jax.numpy as jnp
from jax import lax
from jax.experimental import pallas as pl
from jax.experimental.pallas import tpu as pltpu
from jax.sharding import PartitionSpec as P

SWEEPS = 3
FIRST_LAG, SECOND_LAG = 2, 4
MESH = pl.DeviceIdType.MESH
UP, DOWN, RIGHT, LEFT = range(4)


def softplus(value):
    return jnp.maximum(value, 0.0) + jnp.log(1.0 + jnp.exp(-jnp.abs(value)))


def harmonic(first_cond, second_cond):
    summed = first_cond + second_cond
    return 2.0 * first_cond * second_cond / jnp.where(summed > 0.0, summed, 1.0)


def kernel(
    sizes,
    tracers_hbm,
    wind_hbm,
    head_hbm,
    storage_hbm,
    type_hbm,
    mask_hbm,
    cond_table,
    exp_table,
    out_hbm,
    head_out_hbm,
    q,
    middle,
    wind,
    row_send,
    row_recv,
    col_send,
    col_recv,
    head,
    storage,
    soil_type,
    mask,
    saturated,
    exponent,
    iterate,
    cond,
    surface_send,
    surface,
    edge_send,
    edge_recv,
    side_send,
    side_recv,
    load_sem,
    soil_sem,
    store_sem,
    send_sem,
    recv_sem,
    edge_send_sem,
    edge_recv_sem,
    surface_sem,
    head_sem,
):
    n_mp, n_gx, n_gy, chunk = sizes
    species, levels, rows, cols = tracers_hbm.shape
    layers, soil_rows, soil_cols = head_hbm.shape
    chunks = levels // chunk
    mp, gx, gy = lax.axis_index("mp"), lax.axis_index("gx"), lax.axis_index("gy")
    across = mp * n_gy + gy
    along = gx * n_gy + gy
    n_across, n_along = n_mp * n_gy, n_gx * n_gy

    def across_device(index):
        return (index // n_gy, gx, lax.rem(index, n_gy))

    def along_device(index):
        return (mp, index // n_gy, lax.rem(index, n_gy))

    sends = (gx < n_gx - 1, gx > 0, across < n_across - 1, across > 0)
    gets = (gx > 0, gx < n_gx - 1, across > 0, across < n_across - 1)
    targets = (
        (mp, gx + 1, gy),
        (mp, gx - 1, gy),
        across_device(across + 1),
        across_device(across - 1),
    )

    def load(c):
        part = pl.ds(c * chunk, chunk)
        return (
            pltpu.make_async_copy(wind_hbm.at[:, part], wind.at[:, part], load_sem.at[0, c]),
            pltpu.make_async_copy(tracers_hbm.at[:, part], q.at[:, part], load_sem.at[1, c]),
        )

    def store(c):
        part = pl.ds(c * chunk, chunk)
        return pltpu.make_async_copy(q.at[:, part], out_hbm.at[:, part], store_sem.at[c])

    for copy in load(0):
        copy.start()

    soil_loads = [
        pltpu.make_async_copy(source, target, soil_sem.at[place])
        for place, (source, target) in enumerate(
            ((head_hbm, head), (storage_hbm, storage), (type_hbm, soil_type), (mask_hbm, mask))
        )
    ]
    for copy in soil_loads:
        copy.start()

    barrier = pltpu.get_barrier_semaphore()
    other_chip = lax.rem(mp + 1, n_mp)
    greeted = list(zip(sends, targets)) + [
        (jnp.logical_and(along > 0, gy == 0), along_device(along - 1)),
        (jnp.logical_and(along < n_along - 1, gy == n_gy - 1), along_device(along + 1)),
        (mp >= 0, (other_chip, gx, gy)),
    ]
    for there, device in greeted:

        @pl.when(there)
        def _(device=device):
            pl.semaphore_signal(barrier, inc=1, device_id=device, device_id_type=MESH)

    @pl.loop(1, chunks)
    def _(c):
        for copy in load(c):
            copy.start()

    pl.semaphore_wait(barrier, sum(there.astype(jnp.int32) for there, _ in greeted))

    def transfer(c, turn, way):
        part = pl.ds(c * chunk, chunk)
        if way < 2:
            source, target = row_send.at[turn, way, part], row_recv.at[turn, way, part]
        else:
            source, target = col_send.at[turn, part], col_recv.at[turn, way - 2, part]
        return pltpu.make_async_remote_copy(
            src_ref=source,
            dst_ref=target,
            send_sem=send_sem.at[turn, way, c],
            recv_sem=recv_sem.at[turn, way, c],
            device_id=targets[way],
            device_id_type=MESH,
        )

    def start(c, turn):
        for way in range(4):

            @pl.when(sends[way])
            def _(way=way):
                transfer(c, turn, way).start()

    def arrive(c, turn):
        for way in range(4):

            @pl.when(gets[way])
            def _(way=way):
                transfer(c, turn, way).wait_recv()

    lane = lax.broadcasted_iota(jnp.int32, (rows, cols), 1)

    even = lax.rem(lane, 2) == 0

    def winds(level):
        u, v = wind[0, level], wind[1, level]
        return jnp.maximum(u, 0.0), jnp.minimum(u, 0.0), jnp.maximum(v, 0.0), jnp.minimum(v, 0.0)

    def pack(level, turn, kind, field, parts, edge_wind, packed):
        u_pos, u_neg = parts[:2]
        last, first = slice(rows - 1, rows), slice(0, 1)
        row_send[turn, UP, level, kind : kind + 1] = u_pos[last] * field[last]
        row_send[turn, DOWN, level, kind : kind + 1] = u_neg[first] * field[first]
        part = edge_wind * field
        if kind > 0:
            part = pltpu.roll(part, 2 * kind, 1)
        return packed + part

    def edge_of(parts):
        return jnp.where(lane == cols - 1, parts[2], jnp.where(lane == 0, parts[3], 0.0))

    def blank():
        return jnp.zeros((rows, cols), jnp.float32)

    def side_halo(level, turn):
        left = pltpu.roll(col_recv[turn, 0, level], 1, 1)
        right = pltpu.roll(col_recv[turn, 1, level], cols - 1, 1)
        return jnp.where(even, left, right)

    def keep_of(parts):
        u_pos, u_neg, v_pos, v_neg = parts
        return (1.0 - (u_pos - u_neg)) - (v_pos - v_neg)

    blocks = rows // 8
    row8 = lax.broadcasted_iota(jnp.int32, (8, cols), 0)

    def advance(level, turn, kind, field, parts, keep, sides):
        u_pos, u_neg, v_pos, v_neg = parts
        plus, minus = u_pos * field, u_neg * field
        plus = [pltpu.roll(plus[8 * b : 8 * b + 8], 1, 0) for b in range(blocks)]
        minus = [pltpu.roll(minus[8 * b : 8 * b + 8], 7, 0) for b in range(blocks)]
        below = [row_recv[turn, UP, level, kind : kind + 1]] + plus
        above = minus + [row_recv[turn, DOWN, level, kind : kind + 1]]
        inflow = jnp.concatenate(
            [
                jnp.where(row8 == 0, below[b], plus[b])
                - jnp.where(row8 == 7, above[b + 1], minus[b])
                for b in range(blocks)
            ],
            axis=0,
        )
        if kind > 0:
            sides = pltpu.roll(sides, cols - 2 * kind, 1)
        right = jnp.where(lane == cols - 1, sides, pltpu.roll(v_neg * field, cols - 1, 1))
        left = jnp.where(lane == 0, sides, pltpu.roll(v_pos * field, 1, 1))
        return keep * field + inflow + (left - right)

    def close_ends():
        for way in range(4):
            place = row_recv if way < 2 else col_recv

            @pl.when(jnp.logical_not(gets[way]))
            def _(place=place, way=way):
                place[:, way % 2] = jnp.zeros_like(place[:, way % 2])

    def first_edges(c):
        @pl.loop(c * chunk, (c + 1) * chunk)
        def _(level):
            parts, packed = winds(level), blank()
            edge_wind = edge_of(parts)
            for kind in range(species):
                packed = pack(level, 0, kind, q[kind, level], parts, edge_wind, packed)
            col_send[0, level] = packed

    def first_step(c):
        @pl.loop(c * chunk, (c + 1) * chunk)
        def _(level):
            parts, packed = winds(level), blank()
            edge_wind, keep, sides = edge_of(parts), keep_of(parts), side_halo(level, 0)
            for kind in range(species):
                field = advance(level, 0, kind, q[kind, level], parts, keep, sides)
                packed = pack(level, 1, kind, field, parts, edge_wind, packed)
                middle[kind, level] = field
            col_send[1, level] = packed

    def second_step(c):
        @pl.loop(c * chunk, (c + 1) * chunk)
        def _(level):
            parts, sides = winds(level), side_halo(level, 1)
            keep = keep_of(parts)
            for kind in range(species):
                q[kind, level] = advance(level, 1, kind, middle[kind, level], parts, keep, sides)

    edge_sends = (along < n_along - 1, along > 0, mp >= 0)
    edge_gets = (along > 0, along < n_along - 1, mp >= 0)
    edge_targets = (along_device(along + 1), along_device(along - 1), (other_chip, gx, gy))
    half = soil_cols // 2

    def edge_transfer(turn, way):
        source, target = (
            (edge_send.at[turn, way], edge_recv.at[turn, way])
            if way < 2
            else (side_send.at[turn], side_recv.at[turn])
        )
        return pltpu.make_async_remote_copy(
            src_ref=source,
            dst_ref=target,
            send_sem=edge_send_sem.at[turn, way],
            recv_sem=edge_recv_sem.at[turn, way],
            device_id=edge_targets[way],
            device_id_type=MESH,
        )

    def soil_edges(turn):
        for layer in range(layers):
            values = iterate[layer]
            conds = saturated[...] * jnp.exp(exponent[...] * jnp.minimum(values, 0.0))
            cond[layer] = conds
            for place, array in enumerate((values, conds)):
                edge_send[turn, 0, place, layer : layer + 1] = array[soil_rows - 1 : soil_rows]
                edge_send[turn, 1, place, layer : layer + 1] = array[0:1]
                side_send[turn, place, layer] = jnp.where(mp == 0, array[:, half:], array[:, :half])
        for way in range(3):

            @pl.when(edge_sends[way])
            def _(way=way):
                edge_transfer(turn, way).start()

    soil_row = lax.broadcasted_iota(jnp.int32, (soil_rows, soil_cols), 0)
    soil_lane = lax.broadcasted_iota(jnp.int32, (soil_rows, soil_cols), 1)

    def soil_sweep(turn):
        for way in range(3):

            @pl.when(edge_gets[way])
            def _(way=way):
                edge_transfer(turn, way).wait_recv()

        def neighbours(place, layer, array):
            low = edge_recv[turn, 0, place, layer : layer + 1]
            high = edge_recv[turn, 1, place, layer : layer + 1]
            side = side_recv[turn, place, layer]
            side = jnp.concatenate([side, side], axis=1)
            left_end = jnp.where(mp == 0, 0.0, pltpu.roll(side, 1, 1))
            right_end = jnp.where(mp == n_mp - 1, 0.0, pltpu.roll(side, soil_cols - 1, 1))
            return (
                jnp.where(soil_row == 0, low, pltpu.roll(array, 1, 0)),
                jnp.where(soil_row == soil_rows - 1, high, pltpu.roll(array, soil_rows - 1, 0)),
                jnp.where(soil_lane == 0, left_end, pltpu.roll(array, 1, 1)),
                jnp.where(soil_lane == soil_cols - 1, right_end, pltpu.roll(array, soil_cols - 1, 1)),
            )

        values = [iterate[layer] for layer in range(layers)]
        below_faces = [harmonic(cond[i], cond[i + 1]) for i in range(layers - 1)]
        for layer in range(layers):
            center = cond[layer]
            capacity = storage[layer]
            top, bottom = capacity * head[layer], capacity
            for near_cond, near in zip(
                neighbours(1, layer, center), neighbours(0, layer, values[layer])
            ):
                face = harmonic(center, near_cond)
                top = top + face * near
                bottom = bottom + face
            if layer > 0:
                face = below_faces[layer - 1]
                top = top + face * values[layer - 1] + face
                bottom = bottom + face
            if layer < layers - 1:
                face = below_faces[layer]
                top = top + face * values[layer + 1] - face
                bottom = bottom + face
            if layer == 0:
                top = top + mask[...].astype(jnp.float32) * surface[...]
            if layer == layers - 1:
                top = top - center
            iterate[layer] = top / bottom

    def soil_start():
        for copy in soil_loads:
            copy.wait()
        kinds = soil_type[...]
        for target, table in ((saturated, cond_table), (exponent, exp_table)):
            found = jnp.zeros(kinds.shape, jnp.float32)
            for kind in range(table.shape[0]):
                found = jnp.where(kinds == kind, table[kind], found)
            target[...] = found
        for way in range(2):

            @pl.when(jnp.logical_not(edge_gets[way]))
            def _(way=way):
                edge_recv[:, way] = jnp.zeros_like(edge_recv[:, way])

        iterate[...] = head[...]
        soil_edges(0)

    def surface_transfer(core):
        return pltpu.make_async_remote_copy(
            src_ref=surface_send,
            dst_ref=surface.at[:, pl.ds(core * cols, cols)],
            send_sem=surface_sem.at[0],
            recv_sem=surface_sem.at[1],
            device_id=(mp, gx, 1 - gy),
            device_id_type=MESH,
        )

    def surface_start():
        precip = softplus(q[3, 0])
        evaporation = softplus(-q[1, 0])
        radiation = jnp.exp(-softplus(q[2, 0])) / (1.0 + jnp.exp(-q[0, 0]))
        field = precip - evaporation * radiation
        for core in range(2):

            @pl.when(gy == core)
            def _(core=core):
                other = 1 - core
                surface[:, core * cols : (core + 1) * cols] = field[
                    core * soil_rows : (core + 1) * soil_rows
                ]
                surface_send[...] = field[other * soil_rows : (other + 1) * soil_rows]
                surface_transfer(core).start()

    def surface_wait():
        for core in range(2):

            @pl.when(gy == core)
            def _(core=core):
                surface_transfer(1 - core).wait_recv()
                surface_transfer(core).wait_send()

    head_store = pltpu.make_async_copy(iterate, head_out_hbm, head_sem.at[0])

    @pl.loop(0, chunks + SECOND_LAG)
    def _(turn):
        @pl.when(turn < chunks)
        def _():
            for copy in load(turn):
                copy.wait()
            first_edges(turn)
            start(turn, 0)

        @pl.when(turn == 0)
        def _():
            close_ends()
            soil_start()

        @pl.when(jnp.logical_and(turn >= FIRST_LAG, turn < chunks + FIRST_LAG))
        def _():
            arrive(turn - FIRST_LAG, 0)
            first_step(turn - FIRST_LAG)
            start(turn - FIRST_LAG, 1)

        @pl.when(turn >= SECOND_LAG)
        def _():
            arrive(turn - SECOND_LAG, 1)
            second_step(turn - SECOND_LAG)
            store(turn - SECOND_LAG).start()

        @pl.when(turn == SECOND_LAG)
        def _():
            surface_start()

        @pl.when(turn == SECOND_LAG + 2)
        def _():
            surface_wait()
            soil_sweep(0)
            soil_edges(1)

        @pl.when(turn == SECOND_LAG + 4)
        def _():
            soil_sweep(1)
            soil_edges(2)

        @pl.when(turn == SECOND_LAG + 6)
        def _():
            soil_sweep(2)
            head_store.start()

    for turn in range(SWEEPS):
        for way in range(3):

            @pl.when(edge_sends[way])
            def _(turn=turn, way=way):
                edge_transfer(turn, way).wait_send()

    head_store.wait()

    @pl.loop(0, chunks)
    def _(c):
        for turn in range(2):
            for way in range(4):

                @pl.when(sends[way])
                def _(turn=turn, way=way):
                    transfer(c, turn, way).wait_send()

        store(c).wait()


def on_device(sizes, *arguments):
    tracers, wind, head = arguments[:3]
    species, levels, rows, cols = tracers.shape
    layers, soil_rows, soil_cols = head.shape
    chunk = next(c for c in (6, 5, 4, 3, 2, 1) if levels % c == 0)
    chunks = levels // chunk
    f32 = jnp.float32
    anywhere = pl.BlockSpec(memory_space=pl.ANY)
    scalars = pl.BlockSpec(memory_space=pltpu.SMEM)
    soil = (layers, soil_rows, soil_cols)
    return pl.pallas_call(
        functools.partial(kernel, sizes + (chunk,)),
        out_shape=(
            jax.ShapeDtypeStruct(tracers.shape, f32),
            jax.ShapeDtypeStruct(head.shape, f32),
        ),
        in_specs=[pl.BlockSpec(memory_space=pltpu.HBM)] * 6 + [scalars] * 2,
        out_specs=(anywhere, anywhere),
        scratch_shapes=[
            pltpu.VMEM(tracers.shape, f32),
            pltpu.VMEM(tracers.shape, f32),
            pltpu.VMEM(wind.shape, f32),
            pltpu.VMEM((2, 2, levels, species, cols), f32),
            pltpu.VMEM((2, 2, levels, species, cols), f32),
            pltpu.VMEM((2, levels, rows, cols), f32),
            pltpu.VMEM((2, 2, levels, rows, cols), f32),
            pltpu.VMEM(soil, f32),
            pltpu.VMEM(soil, f32),
            pltpu.VMEM(soil[1:], jnp.int32),
            pltpu.VMEM(soil[1:], jnp.int32),
            pltpu.VMEM(soil[1:], f32),
            pltpu.VMEM(soil[1:], f32),
            pltpu.VMEM(soil, f32),
            pltpu.VMEM(soil, f32),
            pltpu.VMEM((soil_rows, cols), f32),
            pltpu.VMEM((soil_rows, soil_cols), f32),
            pltpu.VMEM((SWEEPS, 2, 2, layers, soil_cols), f32),
            pltpu.VMEM((SWEEPS, 2, 2, layers, soil_cols), f32),
            pltpu.VMEM((SWEEPS, 2, layers, soil_rows, soil_cols // 2), f32),
            pltpu.VMEM((SWEEPS, 2, layers, soil_rows, soil_cols // 2), f32),
            pltpu.SemaphoreType.DMA((2, chunks)),
            pltpu.SemaphoreType.DMA((4,)),
            pltpu.SemaphoreType.DMA((chunks,)),
            pltpu.SemaphoreType.DMA((2, 4, chunks)),
            pltpu.SemaphoreType.DMA((2, 4, chunks)),
            pltpu.SemaphoreType.DMA((SWEEPS, 3)),
            pltpu.SemaphoreType.DMA((SWEEPS, 3)),
            pltpu.SemaphoreType.DMA((2,)),
            pltpu.SemaphoreType.DMA((1,)),
        ],
        compiler_params=pltpu.CompilerParams(
            collective_id=0, has_side_effects=True, vmem_limit_bytes=36 * 1024 * 1024
        ),
    )(*[pltpu.with_memory_space_constraint(a, pltpu.HBM) for a in arguments])


def solution(mesh):
    tall, flat = P(None, None, "gx", ("mp", "gy")), P(None, ("gx", "gy"), "mp")
    ground = P(("gx", "gy"), "mp")
    sizes = (mesh.shape["mp"], mesh.shape["gx"], mesh.shape["gy"])
    return jax.shard_map(
        functools.partial(on_device, sizes),
        mesh=mesh,
        in_specs=(tall, tall, flat, flat, ground, ground, P(), P()),
        out_specs=(tall, flat),
        check_vma=False,
    )
```

```python
import functools

import jax
import jax.numpy as jnp
from jax import lax
from jax.experimental import pallas as pl
from jax.experimental.pallas import tpu as pltpu
from jax.sharding import PartitionSpec as P

SWEEPS = 3
FIRST_LAG, SECOND_LAG = 2, 4
MESH = pl.DeviceIdType.MESH
UP, DOWN, RIGHT, LEFT = range(4)


def softplus(value):
    return jnp.maximum(value, 0.0) + jnp.log(1.0 + jnp.exp(-jnp.abs(value)))


def harmonic(first_cond, second_cond):
    summed = first_cond + second_cond
    return 2.0 * first_cond * second_cond / jnp.where(summed > 0.0, summed, 1.0)


def kernel(
    sizes,
    tracers_hbm,
    wind_hbm,
    head_hbm,
    storage_hbm,
    type_hbm,
    mask_hbm,
    cond_table_hbm,
    exp_table_hbm,
    out_hbm,
    head_out_hbm,
    q,
    middle,
    wind,
    row_send,
    row_recv,
    col_send,
    col_recv,
    cond_table,
    exp_table,
    head,
    storage,
    soil_type,
    mask,
    saturated,
    exponent,
    iterate,
    cond,
    surface_send,
    surface,
    edge_send,
    edge_recv,
    side_send,
    side_recv,
    load_sem,
    soil_sem,
    store_sem,
    send_sem,
    recv_sem,
    edge_send_sem,
    edge_recv_sem,
    surface_sem,
    head_sem,
):
    n_mp, n_gx, n_gy, chunk = sizes
    species, levels, rows, cols = tracers_hbm.shape
    layers, soil_rows, soil_cols = head_hbm.shape
    chunks = levels // chunk
    mp, gx, gy = lax.axis_index("mp"), lax.axis_index("gx"), lax.axis_index("gy")
    across = mp * n_gy + gy
    along = gx * n_gy + gy
    n_across, n_along = n_mp * n_gy, n_gx * n_gy

    def across_device(index):
        return (index // n_gy, gx, lax.rem(index, n_gy))

    def along_device(index):
        return (mp, index // n_gy, lax.rem(index, n_gy))

    sends = (gx < n_gx - 1, gx > 0, across < n_across - 1, across > 0)
    gets = (gx > 0, gx < n_gx - 1, across > 0, across < n_across - 1)
    targets = (
        (mp, gx + 1, gy),
        (mp, gx - 1, gy),
        across_device(across + 1),
        across_device(across - 1),
    )

    def load(c):
        part = pl.ds(c * chunk, chunk)
        return (
            pltpu.make_async_copy(wind_hbm.at[:, part], wind.at[:, part], load_sem.at[0, c]),
            pltpu.make_async_copy(tracers_hbm.at[:, part], q.at[:, part], load_sem.at[1, c]),
        )

    def store(c):
        part = pl.ds(c * chunk, chunk)
        return pltpu.make_async_copy(q.at[:, part], out_hbm.at[:, part], store_sem.at[c])

    for copy in load(0):
        copy.start()

    soil_loads = [
        pltpu.make_async_copy(source, target, soil_sem.at[place])
        for place, (source, target) in enumerate(
            (
                (head_hbm, head),
                (storage_hbm, storage),
                (type_hbm, soil_type),
                (mask_hbm, mask),
                (cond_table_hbm, cond_table),
                (exp_table_hbm, exp_table),
            )
        )
    ]
    for copy in soil_loads:
        copy.start()

    barrier = pltpu.get_barrier_semaphore()
    other_chip = lax.rem(mp + 1, n_mp)
    greeted = list(zip(sends, targets)) + [
        (jnp.logical_and(along > 0, gy == 0), along_device(along - 1)),
        (jnp.logical_and(along < n_along - 1, gy == n_gy - 1), along_device(along + 1)),
        (mp >= 0, (other_chip, gx, gy)),
    ]
    for there, device in greeted:

        @pl.when(there)
        def _(device=device):
            pl.semaphore_signal(barrier, inc=1, device_id=device, device_id_type=MESH)

    @pl.loop(1, chunks)
    def _(c):
        for copy in load(c):
            copy.start()

    pl.semaphore_wait(barrier, sum(there.astype(jnp.int32) for there, _ in greeted))

    def transfer(c, turn, way):
        part = pl.ds(c * chunk, chunk)
        if way < 2:
            source, target = row_send.at[turn, way, part], row_recv.at[turn, way, part]
        else:
            source, target = col_send.at[turn, part], col_recv.at[turn, way - 2, part]
        return pltpu.make_async_remote_copy(
            src_ref=source,
            dst_ref=target,
            send_sem=send_sem.at[turn, way, c],
            recv_sem=recv_sem.at[turn, way, c],
            device_id=targets[way],
            device_id_type=MESH,
        )

    def start(c, turn):
        for way in range(4):

            @pl.when(sends[way])
            def _(way=way):
                transfer(c, turn, way).start()

    def arrive(c, turn):
        for way in range(4):

            @pl.when(gets[way])
            def _(way=way):
                transfer(c, turn, way).wait_recv()

    lane = lax.broadcasted_iota(jnp.int32, (rows, cols), 1)

    even = lax.rem(lane, 2) == 0

    def winds(level):
        u, v = wind[0, level], wind[1, level]
        return jnp.maximum(u, 0.0), jnp.minimum(u, 0.0), jnp.maximum(v, 0.0), jnp.minimum(v, 0.0)

    def pack(level, turn, kind, field, parts, edge_wind, packed):
        u_pos, u_neg = parts[:2]
        last, first = slice(rows - 1, rows), slice(0, 1)
        row_send[turn, UP, level, kind : kind + 1] = u_pos[last] * field[last]
        row_send[turn, DOWN, level, kind : kind + 1] = u_neg[first] * field[first]
        part = edge_wind * field
        if kind > 0:
            part = pltpu.roll(part, 2 * kind, 1)
        return packed + part

    def edge_of(parts):
        return jnp.where(lane == cols - 1, parts[2], jnp.where(lane == 0, parts[3], 0.0))

    def blank():
        return jnp.zeros((rows, cols), jnp.float32)

    def side_halo(level, turn):
        left = pltpu.roll(col_recv[turn, 0, level], 1, 1)
        right = pltpu.roll(col_recv[turn, 1, level], cols - 1, 1)
        return jnp.where(even, left, right)

    def keep_of(parts):
        u_pos, u_neg, v_pos, v_neg = parts
        return (1.0 - (u_pos - u_neg)) - (v_pos - v_neg)

    blocks = rows // 8
    row8 = lax.broadcasted_iota(jnp.int32, (8, cols), 0)

    def advance(level, turn, kind, field, parts, keep, sides):
        u_pos, u_neg, v_pos, v_neg = parts
        plus, minus = u_pos * field, u_neg * field
        plus = [pltpu.roll(plus[8 * b : 8 * b + 8], 1, 0) for b in range(blocks)]
        minus = [pltpu.roll(minus[8 * b : 8 * b + 8], 7, 0) for b in range(blocks)]
        below = [row_recv[turn, UP, level, kind : kind + 1]] + plus
        above = minus + [row_recv[turn, DOWN, level, kind : kind + 1]]
        inflow = jnp.concatenate(
            [
                jnp.where(row8 == 0, below[b], plus[b])
                - jnp.where(row8 == 7, above[b + 1], minus[b])
                for b in range(blocks)
            ],
            axis=0,
        )
        if kind > 0:
            sides = pltpu.roll(sides, cols - 2 * kind, 1)
        right = jnp.where(lane == cols - 1, sides, pltpu.roll(v_neg * field, cols - 1, 1))
        left = jnp.where(lane == 0, sides, pltpu.roll(v_pos * field, 1, 1))
        return keep * field + inflow + (left - right)

    def close_ends():
        for way in range(4):
            place = row_recv if way < 2 else col_recv

            @pl.when(jnp.logical_not(gets[way]))
            def _(place=place, way=way):
                place[:, way % 2] = jnp.zeros_like(place[:, way % 2])

    def first_edges(c):
        @pl.loop(c * chunk, (c + 1) * chunk)
        def _(level):
            parts, packed = winds(level), blank()
            edge_wind = edge_of(parts)
            for kind in range(species):
                packed = pack(level, 0, kind, q[kind, level], parts, edge_wind, packed)
            col_send[0, level] = packed

    def first_step(c):
        @pl.loop(c * chunk, (c + 1) * chunk)
        def _(level):
            parts, packed = winds(level), blank()
            edge_wind, keep, sides = edge_of(parts), keep_of(parts), side_halo(level, 0)
            for kind in range(species):
                field = advance(level, 0, kind, q[kind, level], parts, keep, sides)
                packed = pack(level, 1, kind, field, parts, edge_wind, packed)
                middle[kind, level] = field
            col_send[1, level] = packed

    def second_step(c):
        @pl.loop(c * chunk, (c + 1) * chunk)
        def _(level):
            parts, sides = winds(level), side_halo(level, 1)
            keep = keep_of(parts)
            for kind in range(species):
                q[kind, level] = advance(level, 1, kind, middle[kind, level], parts, keep, sides)

    edge_sends = (along < n_along - 1, along > 0, mp >= 0)
    edge_gets = (along > 0, along < n_along - 1, mp >= 0)
    edge_targets = (along_device(along + 1), along_device(along - 1), (other_chip, gx, gy))
    half = soil_cols // 2

    def edge_transfer(turn, way):
        source, target = (
            (edge_send.at[turn, way], edge_recv.at[turn, way])
            if way < 2
            else (side_send.at[turn], side_recv.at[turn])
        )
        return pltpu.make_async_remote_copy(
            src_ref=source,
            dst_ref=target,
            send_sem=edge_send_sem.at[turn, way],
            recv_sem=edge_recv_sem.at[turn, way],
            device_id=edge_targets[way],
            device_id_type=MESH,
        )

    def soil_edges(turn):
        for layer in range(layers):
            values = iterate[layer]
            conds = saturated[...] * jnp.exp(exponent[...] * jnp.minimum(values, 0.0))
            cond[layer] = conds
            for place, array in enumerate((values, conds)):
                edge_send[turn, 0, place, layer : layer + 1] = array[soil_rows - 1 : soil_rows]
                edge_send[turn, 1, place, layer : layer + 1] = array[0:1]
                side_send[turn, place, layer] = jnp.where(mp == 0, array[:, half:], array[:, :half])
        for way in range(3):

            @pl.when(edge_sends[way])
            def _(way=way):
                edge_transfer(turn, way).start()

    soil_row = lax.broadcasted_iota(jnp.int32, (soil_rows, soil_cols), 0)
    soil_lane = lax.broadcasted_iota(jnp.int32, (soil_rows, soil_cols), 1)

    def soil_sweep(turn):
        for way in range(3):

            @pl.when(edge_gets[way])
            def _(way=way):
                edge_transfer(turn, way).wait_recv()

        def neighbours(place, layer, array):
            low = edge_recv[turn, 0, place, layer : layer + 1]
            high = edge_recv[turn, 1, place, layer : layer + 1]
            side = side_recv[turn, place, layer]
            side = jnp.concatenate([side, side], axis=1)
            left_end = jnp.where(mp == 0, 0.0, pltpu.roll(side, 1, 1))
            right_end = jnp.where(mp == n_mp - 1, 0.0, pltpu.roll(side, soil_cols - 1, 1))
            return (
                jnp.where(soil_row == 0, low, pltpu.roll(array, 1, 0)),
                jnp.where(soil_row == soil_rows - 1, high, pltpu.roll(array, soil_rows - 1, 0)),
                jnp.where(soil_lane == 0, left_end, pltpu.roll(array, 1, 1)),
                jnp.where(soil_lane == soil_cols - 1, right_end, pltpu.roll(array, soil_cols - 1, 1)),
            )

        values = [iterate[layer] for layer in range(layers)]
        below_faces = [harmonic(cond[i], cond[i + 1]) for i in range(layers - 1)]
        for layer in range(layers):
            center = cond[layer]
            capacity = storage[layer]
            top, bottom = capacity * head[layer], capacity
            for near_cond, near in zip(
                neighbours(1, layer, center), neighbours(0, layer, values[layer])
            ):
                face = harmonic(center, near_cond)
                top = top + face * near
                bottom = bottom + face
            if layer > 0:
                face = below_faces[layer - 1]
                top = top + face * values[layer - 1] + face
                bottom = bottom + face
            if layer < layers - 1:
                face = below_faces[layer]
                top = top + face * values[layer + 1] - face
                bottom = bottom + face
            if layer == 0:
                top = top + mask[...].astype(jnp.float32) * surface[...]
            if layer == layers - 1:
                top = top - center
            iterate[layer] = top / bottom

    def soil_start():
        for copy in soil_loads:
            copy.wait()
        kinds = soil_type[...]
        for target, table in ((saturated, cond_table), (exponent, exp_table)):
            found = jnp.zeros(kinds.shape, jnp.float32)
            for kind in range(table.shape[0]):
                found = jnp.where(kinds == kind, table[kind], found)
            target[...] = found
        for way in range(2):

            @pl.when(jnp.logical_not(edge_gets[way]))
            def _(way=way):
                edge_recv[:, way] = jnp.zeros_like(edge_recv[:, way])

        iterate[...] = head[...]
        soil_edges(0)

    def surface_transfer(core):
        return pltpu.make_async_remote_copy(
            src_ref=surface_send,
            dst_ref=surface.at[:, pl.ds(core * cols, cols)],
            send_sem=surface_sem.at[0],
            recv_sem=surface_sem.at[1],
            device_id=(mp, gx, 1 - gy),
            device_id_type=MESH,
        )

    def surface_start():
        precip = softplus(q[3, 0])
        evaporation = softplus(-q[1, 0])
        radiation = jnp.exp(-softplus(q[2, 0])) / (1.0 + jnp.exp(-q[0, 0]))
        field = precip - evaporation * radiation
        for core in range(2):

            @pl.when(gy == core)
            def _(core=core):
                other = 1 - core
                surface[:, core * cols : (core + 1) * cols] = field[
                    core * soil_rows : (core + 1) * soil_rows
                ]
                surface_send[...] = field[other * soil_rows : (other + 1) * soil_rows]
                surface_transfer(core).start()

    def surface_wait():
        for core in range(2):

            @pl.when(gy == core)
            def _(core=core):
                surface_transfer(1 - core).wait_recv()
                surface_transfer(core).wait_send()

    head_store = pltpu.make_async_copy(iterate, head_out_hbm, head_sem.at[0])

    @pl.loop(0, chunks + SECOND_LAG)
    def _(turn):
        @pl.when(turn < chunks)
        def _():
            for copy in load(turn):
                copy.wait()
            first_edges(turn)
            start(turn, 0)

        @pl.when(turn == 1)
        def _():
            close_ends()
            soil_start()

        @pl.when(jnp.logical_and(turn >= FIRST_LAG, turn < chunks + FIRST_LAG))
        def _():
            arrive(turn - FIRST_LAG, 0)
            first_step(turn - FIRST_LAG)
            start(turn - FIRST_LAG, 1)

        @pl.when(turn >= SECOND_LAG)
        def _():
            arrive(turn - SECOND_LAG, 1)
            second_step(turn - SECOND_LAG)
            store(turn - SECOND_LAG).start()

        @pl.when(turn == SECOND_LAG)
        def _():
            surface_start()

        @pl.when(turn == SECOND_LAG + 2)
        def _():
            surface_wait()
            soil_sweep(0)
            soil_edges(1)

        @pl.when(turn == SECOND_LAG + 4)
        def _():
            soil_sweep(1)
            soil_edges(2)

        @pl.when(turn == SECOND_LAG + 6)
        def _():
            soil_sweep(2)
            head_store.start()

    for turn in range(SWEEPS):
        for way in range(3):

            @pl.when(edge_sends[way])
            def _(turn=turn, way=way):
                edge_transfer(turn, way).wait_send()

    head_store.wait()

    @pl.loop(0, chunks)
    def _(c):
        for turn in range(2):
            for way in range(4):

                @pl.when(sends[way])
                def _(turn=turn, way=way):
                    transfer(c, turn, way).wait_send()

        store(c).wait()


def on_device(sizes, *arguments):
    tracers, wind, head = arguments[:3]
    species, levels, rows, cols = tracers.shape
    layers, soil_rows, soil_cols = head.shape
    chunk = next(c for c in (6, 5, 4, 3, 2, 1) if levels % c == 0)
    chunks = levels // chunk
    f32 = jnp.float32
    anywhere = pl.BlockSpec(memory_space=pl.ANY)
    soil = (layers, soil_rows, soil_cols)
    return pl.pallas_call(
        functools.partial(kernel, sizes + (chunk,)),
        out_shape=(
            jax.ShapeDtypeStruct(tracers.shape, f32),
            jax.ShapeDtypeStruct(head.shape, f32),
        ),
        in_specs=[pl.BlockSpec(memory_space=pltpu.HBM)] * 8,
        out_specs=(anywhere, anywhere),
        scratch_shapes=[
            pltpu.VMEM(tracers.shape, f32),
            pltpu.VMEM(tracers.shape, f32),
            pltpu.VMEM(wind.shape, f32),
            pltpu.VMEM((2, 2, levels, species, cols), f32),
            pltpu.VMEM((2, 2, levels, species, cols), f32),
            pltpu.VMEM((2, levels, rows, cols), f32),
            pltpu.VMEM((2, 2, levels, rows, cols), f32),
            pltpu.SMEM(arguments[6].shape, f32),
            pltpu.SMEM(arguments[7].shape, f32),
            pltpu.VMEM(soil, f32),
            pltpu.VMEM(soil, f32),
            pltpu.VMEM(soil[1:], jnp.int32),
            pltpu.VMEM(soil[1:], jnp.int32),
            pltpu.VMEM(soil[1:], f32),
            pltpu.VMEM(soil[1:], f32),
            pltpu.VMEM(soil, f32),
            pltpu.VMEM(soil, f32),
            pltpu.VMEM((soil_rows, cols), f32),
            pltpu.VMEM((soil_rows, soil_cols), f32),
            pltpu.VMEM((SWEEPS, 2, 2, layers, soil_cols), f32),
            pltpu.VMEM((SWEEPS, 2, 2, layers, soil_cols), f32),
            pltpu.VMEM((SWEEPS, 2, layers, soil_rows, soil_cols // 2), f32),
            pltpu.VMEM((SWEEPS, 2, layers, soil_rows, soil_cols // 2), f32),
            pltpu.SemaphoreType.DMA((2, chunks)),
            pltpu.SemaphoreType.DMA((6,)),
            pltpu.SemaphoreType.DMA((chunks,)),
            pltpu.SemaphoreType.DMA((2, 4, chunks)),
            pltpu.SemaphoreType.DMA((2, 4, chunks)),
            pltpu.SemaphoreType.DMA((SWEEPS, 3)),
            pltpu.SemaphoreType.DMA((SWEEPS, 3)),
            pltpu.SemaphoreType.DMA((2,)),
            pltpu.SemaphoreType.DMA((1,)),
        ],
        compiler_params=pltpu.CompilerParams(
            collective_id=0, has_side_effects=True, vmem_limit_bytes=36 * 1024 * 1024
        ),
    )(*[pltpu.with_memory_space_constraint(a, pltpu.HBM) for a in arguments])


def solution(mesh):
    tall, flat = P(None, None, "gx", ("mp", "gy")), P(None, ("gx", "gy"), "mp")
    ground = P(("gx", "gy"), "mp")
    sizes = (mesh.shape["mp"], mesh.shape["gx"], mesh.shape["gy"])
    return jax.shard_map(
        functools.partial(on_device, sizes),
        mesh=mesh,
        in_specs=(tall, tall, flat, flat, ground, ground, P(), P()),
        out_specs=(tall, flat),
        check_vma=False,
    )
```
